32 devices in a mesh: runs: 2 (over y), horiz: 4 (over z), comp: 2 (over x), vert: 2 (over core).
Axes of the slice: x: 2, y: 2, z: 4, core: 2. Of those that a mesh axis runs over, the one named last changes fastest.
Arguments:
- atm_state: float32 [128, 128, 512], P('vert', ('runs', 'comp'), 'horiz'), parts along dimension 1, may hold values from -6 to 6
- atm_coeffs: float32 [4, 128], P(None, 'vert'), may hold values from 0.02 to 0.25, as said below
- ocean_state: float32 [80, 64, 512], P('vert', ('runs', 'comp'), 'horiz'), parts along dimension 1, may hold values from -6 to 6
- ocean_coeffs: float32 [4, 80], P(None, 'vert'), may hold values from 0.02 to 0.25, as said below
- atm_flux: bfloat16 [8, 256, 128], P('vert', ('runs', 'horiz', 'comp')), parts along dimension 1, may hold values from -6 to 6
- remap_weights: bfloat16 [32, 128, 128], replicated, may hold values from -0.5 to 0.5
- remap_list: int32 [8, 8, 3], replicated, may hold values from 0 to 127, as said below
- ocean_mask: int32 [64, 128], P(('horiz', 'comp')), may hold values 0 or 1
Outputs:
- atm_final: float32 [128, 128, 512], P('vert', ('runs', 'comp'), 'horiz'), parts along dimension 1
- ocean_final: float32 [80, 64, 512], P('vert', ('runs', 'comp'), 'horiz'), parts along dimension 1
- remapped: float32 [8, 128, 128], P('vert', ('runs', 'horiz', 'comp')), parts along dimension 1
The draws below stay inside these ranges and needn't reach their ends.
There are 2 independent parts, one for each index of `runs`. The reference program is written for one: setup_inputs(seed, part) draws one part's arguments, and reference() takes and returns one part's arrays. A program takes and returns all parts, laid end to end along the dimension named above; an argument that names none is the same for every part. Nothing has to cross between parts.
Inputs may be any that keep to these rules, and one draw needn't show every extreme that they name: `remap_list`: row p lists the entries whose destination blocks are p * 8 to (p + 1) * 8 - 1. In every row at most 2 entries have source blocks of one device (blocks d * 16 to (d + 1) * 16 - 1), and in every row some device has exactly 2. Weight block indices lie in 0 to 31. `atm_coeffs`: row 0 and row 1 lie in 0.05 to 0.25, row 2 in 0.02 to 0.08, row 3 in 0.03 to 0.15. `ocean_coeffs`: row 0 and row 1 lie in 0.05 to 0.25, row 2 in 0.02 to 0.08, row 3 in 0.03 to 0.15.
All inputs are finite; a program needn't handle non-finite values. No bound on the sum of `ocean_mask` on one device may be relied on, other than what follows from the above.
Results may differ from the reference program's by a relative error of at most 0.0003.
Values may be sent and summed in bfloat16 or wider, within the bound.
A program may use at most 64 MiB of HBM per device.

```python
import jax
import jax.numpy as jnp
from jax import lax

LEV_A = 128
LEV_O = 80
STEPS = 4
FLUX = 8
BS = 128
NBA_DEV = 16
NBO_DEV = 8
NW = 32
PEERS = 8
E_DEV = 8
NBA = 128
NBO = 64
AY = 64
OY = 32
AX = 512


def coefficient_rows(key, levels):
    unit_draw = jax.random.uniform(key, (4, levels), jnp.float32)
    lower_bound = jnp.array([0.05, 0.05, 0.02, 0.03], jnp.float32)[:, None]
    upper_bound = jnp.array([0.25, 0.25, 0.08, 0.15], jnp.float32)[:, None]
    return lower_bound + (upper_bound - lower_bound) * unit_draw


def draw_atm_coeffs(key, part):
    key = jax.random.fold_in(key, 3)
    return coefficient_rows(key, LEV_A)


def draw_ocean_coeffs(key, part):
    key = jax.random.fold_in(key, 5)
    return coefficient_rows(key, LEV_O)


def draw_remap_list(key, part):
    key = jax.random.fold_in(key, 7)
    key_order, key_shuffle, key_block, key_weight = jax.random.split(key, 4)
    source_order = jax.vmap(lambda subkey: jax.random.permutation(subkey, PEERS))(jax.random.split(key_order, PEERS))
    picked = jnp.arange(E_DEV, dtype=jnp.int32)
    picked = jnp.where(picked < E_DEV // 2, picked // 2, picked)
    source_device = source_order[:, picked]
    shuffle = jax.vmap(lambda subkey: jax.random.permutation(subkey, E_DEV))(jax.random.split(key_shuffle, PEERS))
    source_device = jnp.take_along_axis(source_device, shuffle, axis=1)
    source_local = jax.random.randint(key_block, (PEERS, E_DEV), 0, NBA_DEV)
    target = jnp.arange(PEERS, dtype=jnp.int32)[:, None] * NBO_DEV + shuffle % NBO_DEV
    weight_index = jax.random.randint(key_weight, (PEERS, E_DEV), 0, NW)
    return jnp.stack([source_device * NBA_DEV + source_local, target, weight_index], axis=-1).astype(jnp.int32)


def set_ends(values, own_key, smallest, top_value):
    spot = [jax.random.randint(jax.random.fold_in(own_key, axis), (), 0, length) for axis, length in enumerate(values.shape)]
    longest = values.shape.index(max(values.shape))
    beside = spot[:longest] + [(spot[longest] + 1) % values.shape[longest]] + spot[longest + 1:]
    return values.at[tuple(spot)].set(smallest).at[tuple(beside)].set(top_value)


def block_scale(own_key, dims, pieces, low, high):
    def one(position, shards_of):
        draws = jax.random.uniform(jax.random.fold_in(jax.random.fold_in(own_key, 6), position), (shards_of,), jnp.float32, low / len(pieces), high / len(pieces))
        return jnp.repeat(jnp.exp(draws), dims[position] // shards_of).reshape((-1,) + (1,) * (len(dims) - position - 1))

    factor_of = one(*pieces[0])
    for cut in pieces[1:]:
        factor_of = factor_of * one(*cut)
    return factor_of


def scatter_about(stream_key, dims, width, bound, shards=(), kind=jnp.bfloat16):
    values = jax.random.normal(stream_key, dims, jnp.float32) * width
    if len(shards) > 0:
        values = block_scale(stream_key, dims, shards, -0.22, 0.18) * values
    return jnp.clip(values, min=-bound, max=bound).astype(kind)


def setup_inputs(seed: int = 0, part: int = 0) -> dict:
    streams_of = jax.random.split(jax.random.key(seed), 9)
    part_keys = jax.random.split(jax.random.fold_in(streams_of[8], part), 9)
    atm_state = scatter_about(part_keys[0], (LEV_A, AY, AX), 1.0, 6.0, ((0, 2), (1, 2), (2, 4)), jnp.float32)
    atm_coeffs = draw_atm_coeffs(jax.random.fold_in(streams_of[8], 71), part)
    ocean_state = scatter_about(part_keys[2], (LEV_O, OY, AX), 1.0, 6.0, ((0, 2), (1, 2), (2, 4)), jnp.float32)
    ocean_coeffs = draw_ocean_coeffs(jax.random.fold_in(streams_of[8], 71), part)
    atm_flux = scatter_about(part_keys[4], (FLUX, NBA, BS), 1.0, 6.0, ((0, 2), (1, 8)))
    remap_weights = scatter_about(streams_of[5], (NW, BS, BS), BS ** -0.5, 0.5)
    remap_list = draw_remap_list(jax.random.fold_in(streams_of[8], 71), part)
    ocean_mask = set_ends((jax.random.randint(streams_of[7], (NBO, BS), 0, 10) < 7).astype(jnp.int32), jax.random.fold_in(streams_of[7], 1), 0, 1)
    return dict(atm_state=atm_state, atm_coeffs=atm_coeffs, ocean_state=ocean_state, ocean_coeffs=ocean_coeffs, atm_flux=atm_flux, remap_weights=remap_weights, remap_list=remap_list, ocean_mask=ocean_mask)


def advance(field, coeffs, levels):
    west_side = jnp.roll(field, 1, axis=2)
    east_side = jnp.roll(field, -1, axis=2)
    south_side = jnp.roll(field, 1, axis=1)
    north_side = jnp.roll(field, -1, axis=1)
    column_mean = jnp.sum(field, axis=0) / levels
    courant_x = coeffs[0][:, None, None]
    courant_y = coeffs[1][:, None, None]
    diffusion = coeffs[2][:, None, None]
    mixing = coeffs[3][:, None, None]
    return (field - courant_x * (field - west_side) - courant_y * (field - south_side)
            + diffusion * (east_side + west_side + north_side + south_side - 4.0 * field)
            - mixing * (field - column_mean[None]))


def remap_blocks(atm_flux, remap_weights, remap_list, ocean_mask):
    def block_row(entries):
        source = entries[:, 0].astype(jnp.int32)
        target = (entries[:, 1] % NBO_DEV).astype(jnp.int32)
        weight_index = entries[:, 2].astype(jnp.int32)
        blocks = jnp.take(atm_flux, source, axis=1).astype(jnp.float32)
        weights = jnp.take(remap_weights, weight_index, axis=0).astype(jnp.float32)
        products = jnp.einsum('fei,eij->efj', blocks, weights)
        dest_hot = (target[None, :] == jnp.arange(NBO_DEV, dtype=jnp.int32)[:, None]).astype(jnp.float32)
        return jnp.einsum('oe,efj->foj', dest_hot, products)

    per_device = lax.map(block_row, remap_list)
    summed = jnp.transpose(per_device, (1, 0, 2, 3)).reshape(FLUX, NBO, BS)
    return summed * ocean_mask.astype(jnp.float32)[None]


def reference(atm_state, atm_coeffs, ocean_state, ocean_coeffs, atm_flux, remap_weights, remap_list, ocean_mask):
    atm_field = atm_state
    ocean_field = ocean_state
    for iteration in range(STEPS):
        atm_field = advance(atm_field, atm_coeffs, LEV_A)
        ocean_field = advance(ocean_field, ocean_coeffs, LEV_O)
    remapped = remap_blocks(atm_flux, remap_weights, remap_list, ocean_mask)
    return atm_field, ocean_field, remapped
```

```python
import functools

import jax
import jax.numpy as jnp
from jax import lax
from jax.experimental import pallas as pl
from jax.experimental.pallas import tpu as pltpu
from jax.sharding import PartitionSpec as P

F32 = jnp.float32
BF16 = jnp.bfloat16
W = 4
ZG = 16 * 8 + 16
G = 16


def rup(x, m):
    return (x + m - 1) // m * m


def lane_iota(rows):
    return lax.broadcasted_iota(jnp.int32, (rows, 128), 1)


def sub_iota(rows):
    return lax.broadcasted_iota(jnp.int32, (rows, 128), 0)


BT = 4


class Field:
    def __init__(self, levels, rows, total, z0, x0, c0, s0):
        self.L, self.R, self.total = levels, rows, total
        self.E = rows + 2 * W
        self.V = (levels + G - 1) // G
        self.full = levels // G
        self.tail = levels - self.full * G
        self.z0, self.x0, self.c0, self.s0 = z0, x0, c0, s0
        self.chunks = [(v, min(G, levels - v * G)) for v in range(self.V)]

    def groups(self, fn):
        if self.full:

            def step(v, carry):
                fn(v, G)
                return carry

            lax.fori_loop(0, self.full, step, 0)
        if self.tail:
            fn(self.full, self.tail)


def kernel(
    fa, fo, NR, H, C, flux_f, nba, entries,
    a_hbm, o_hbm, w_hbm, flux_ref, ac, oc, rl,
    ua_hbm, uo_hbm, ma_ref, mo_ref, rem_ref,
    a_own, o_own, a_ext, o_ext, a_w, a_e, o_w, o_e, a_cl, o_cl,
    a_sum, o_sum, wbuf,
    zs, zr, xf, xs, xr, cs, cr,
    a_vs, a_vr, o_vs, o_vr, a_us, a_ur, o_us, o_ur,
    sel, rs, rr,
    ld_sem, out_sem, z_ss, z_rs, x_ss, x_rs, c_ss, c_rs, v_ss, v_rs, r_ss, r_rs,
):
    def listed(p, e, i):
        return rl[i, p, e]

    hi = lax.axis_index("horiz")
    ci = lax.axis_index("comp")
    vi = lax.axis_index("vert")
    peers = H * C
    me = hi * C + ci
    west, east = lax.rem(hi + H - 1, H), lax.rem(hi + 1, H)
    north, south = lax.rem(ci + 1, C), lax.rem(ci + C - 1, C)
    other = 1 - vi
    MESH = pl.DeviceIdType.MESH

    loads = [
        pltpu.make_async_copy(a_hbm, a_own, ld_sem.at[0]),
        pltpu.make_async_copy(o_hbm, o_own, ld_sem.at[1]),
        pltpu.make_async_copy(w_hbm, wbuf, ld_sem.at[2]),
    ]
    for load in loads:
        load.start()

    barrier = pltpu.get_barrier_semaphore()

    def greet(k, carry):
        peer = lax.rem(me + k, peers)
        pl.semaphore_signal(
            barrier, inc=1, device_id={"horiz": peer // C, "comp": lax.rem(peer, C)}, device_id_type=MESH
        )
        return carry

    pl.semaphore_signal(barrier, inc=1, device_id={"vert": other}, device_id_type=MESH)
    lax.fori_loop(1, peers, greet, 0)

    def scalars(co, l):
        cx, cy, kd, km = co[0, l], co[1, l], co[2, l], co[3, l]
        return 1.0 - cx - cy - 4.0 * kd - km, cx + kd, cy + kd, kd, km

    lane1 = lane_iota(1)

    def spread(f, co, cl):
        def group(v, n):
            rows = [jnp.zeros((1, 128), F32) for _ in range(5)]
            for k in range(n):
                here = (lane1 // 8) == k
                rows = [jnp.where(here, s, r) for s, r in zip(scalars(co, v * G + k), rows)]
            for i in range(5):
                cl[v, i : i + 1, :] = rows[i]

        f.groups(group)

    spread(fa, ac, a_cl)
    spread(fo, oc, o_cl)

    def total_km(f, co):
        def add(l, s):
            return s + co[3, l]

        return lax.fori_loop(0, f.L, add, jnp.float32(0))

    a_k = total_km(fa, ac)
    o_k = total_km(fo, oc)

    sub8 = sub_iota(8)
    sub16 = sub_iota(16)

    def pack(f, own):
        lane = lane_iota(f.R)

        def group(v, n):
            acc = jnp.zeros((f.R, 128), F32)
            z_prev = None
            lost = jnp.zeros((16, 128), F32)
            for k in range(n):
                q = own[v * G + k]
                acc = jnp.where((lane // 8) == k, pltpu.roll(q, (8 * k + 4) % 128, 1), acc)
                z = jnp.where(sub8 < W, q[0:8], q[f.R - 8 : f.R])
                top = q[f.R - 1 : f.R]
                lost = jnp.where(sub16 == k, top - top.astype(BF16).astype(F32), lost)
                if k % 2 == 0:
                    z_prev = z
                else:
                    at = pl.multiple_of(f.z0 + v * ZG + (k - 1) * 8, 16)
                    zs[pl.ds(at, 16), :] = jnp.concatenate([z_prev, z], axis=0).astype(BF16)
            at = pl.multiple_of(f.z0 + v * ZG + n * 8, 16)
            zs[pl.ds(at, 16), :] = lost.astype(BF16)
            at = pl.multiple_of(f.x0 + v * f.R, 16)
            xf[pl.ds(at, f.R), :] = acc
            xs[pl.ds(at, f.R), :] = acc.astype(BF16)

        f.groups(group)
        for v in range(0, rup(f.V, 2), 2):
            parts = []
            for u in (v, v + 1):
                if u < f.V:
                    base = f.x0 + u * f.R
                    parts.append(
                        jnp.where(sub8 < W, xf[base : base + 8, :], xf[base + f.R - 8 : base + f.R, :])
                    )
                else:
                    parts.append(jnp.zeros((8, 128), F32))
            at = f.c0 + v * 8
            cs[at : at + 16, :] = jnp.concatenate(parts, axis=0).astype(BF16)

    row_nbrs = [north] if NR == 1 else [north, south]

    def slot_at(n):
        return n if NR == 1 else 1 - n

    def z_copy(f, n, i, base):
        v, cnt = f.chunks[i]
        at, size = f.z0 + v * ZG, cnt * 8 + 16
        return pltpu.make_async_remote_copy(
            src_ref=zs.at[pl.ds(at, size)],
            dst_ref=zr.at[slot_at(n), pl.ds(at, size)],
            send_sem=z_ss.at[n, base + i],
            recv_sem=z_rs.at[slot_at(n), base + i],
            device_id={"comp": row_nbrs[n]},
            device_id_type=MESH,
        )

    def x_copy(side):
        return pltpu.make_async_remote_copy(
            src_ref=xs,
            dst_ref=xr.at[1 - side],
            send_sem=x_ss.at[side],
            recv_sem=x_rs.at[1 - side],
            device_id={"horiz": west if side == 0 else east},
            device_id_type=MESH,
        )

    def c_copy(n, j):
        col = (west, hi, east)[j]
        return pltpu.make_async_remote_copy(
            src_ref=cs,
            dst_ref=cr.at[slot_at(n), 2 - j],
            send_sem=c_ss.at[n, j],
            recv_sem=c_rs.at[slot_at(n), 2 - j],
            device_id={"horiz": col, "comp": row_nbrs[n]},
            device_id_type=MESH,
        )

    oz = fa.V
    loads[0].wait()
    pack(fa, a_own)
    pl.semaphore_wait(barrier, peers)
    for i in range(fa.V):
        for n in range(NR):
            z_copy(fa, n, i, 0).start()
    loads[1].wait()
    pack(fo, o_own)
    for side in range(2):
        x_copy(side).start()
    for n in range(NR):
        for j in range(3):
            c_copy(n, j).start()
    for i in range(fo.V):
        for n in range(NR):
            z_copy(fo, n, i, oz).start()

    lane8 = lane_iota(8)

    def choose(p, carry):
        first, last = jnp.int32(0), jnp.int32(0)
        seen = jnp.int32(0)

        def look(e, st):
            first, last, seen = st
            s = listed(p, e, 0)
            here = (s // nba) == me
            b = lax.rem(s, nba)
            first = jnp.where(jnp.logical_and(here, seen == 0), b, first)
            last = jnp.where(here, b, last)
            seen = jnp.where(here, 1, seen)
            return first, last, seen

        if entries <= 16:
            st = (first, last, seen)
            for e in range(entries):
                st = look(e, st)
        else:
            st = lax.fori_loop(0, entries, look, (first, last, seen))
        first, last, _ = st
        want = jnp.where(sub8 < flux_f, first, last) + lax.rem(sub8, flux_f) * nba
        at = pl.multiple_of(p * 8, 8)
        sel[pl.ds(at, 8), :] = jnp.where(lane8 == want, 1.0, 0.0)
        return carry

    lax.fori_loop(0, peers, choose, 0)
    depth = flux_f * nba
    picked = jnp.dot(
        sel[:, 0:depth].astype(BF16),
        flux_ref[...].reshape(depth, 128),
        preferred_element_type=F32,
    )
    rs[...] = picked.reshape(peers, 8, 128)
    rr[me] = rs[me]

    def r_copy(k):
        peer = lax.rem(me + k, peers)
        return pltpu.make_async_remote_copy(
            src_ref=rs.at[peer],
            dst_ref=rr.at[me],
            send_sem=r_ss.at[k],
            recv_sem=r_rs.at[k],
            device_id={"horiz": peer // C, "comp": lax.rem(peer, C)},
            device_id_type=MESH,
        )

    def r_start(k, carry):
        r_copy(k).start()
        return carry

    lax.fori_loop(1, peers, r_start, 0)

    def stencil(E, q, wv, ev, a, b, c, d):
        return a * q + b * wv + c * pltpu.roll(q, 1, 0) + d * (ev + pltpu.roll(q, E - 1, 0))

    def one_pass(f, co, cl, own, ext, wt, et, sums, mean, first=False, last=False, after=None):
        E, R = f.E, f.R
        lane = lane_iota(E)
        low = lax.rem(lane, 8) < W
        is0, is127 = lane == 0, lane == 127
        oz_f = 0 if f is fa else fa.V
        nsum = 6 if first else 3
        if not last:
            sums[...] = jnp.zeros_like(sums)

        def rows_of(ref, idx, at):
            t = ref[idx + (pl.ds(pl.multiple_of(at - lax.rem(at, 16), 16), 16), slice(None))].astype(F32)
            return t

        def group(v, n):
            cc = [cl[v, i : i + 1, :] for i in range(5)]
            if first:
                for m in range(NR):
                    size = n * 8 + 16
                    at = f.z0 + v * ZG
                    at = at if isinstance(at, int) else pl.multiple_of(at, 16)
                    pltpu.make_async_remote_copy(
                        src_ref=zs.at[pl.ds(at, size)],
                        dst_ref=zr.at[m, pl.ds(at, size)],
                        send_sem=z_ss.at[m, oz_f + v],
                        recv_sem=z_rs.at[m, oz_f + v],
                        device_id={"comp": row_nbrs[m]},
                        device_id_type=MESH,
                    ).wait_recv()
                xat = f.x0 + v * R
                xat = xat if isinstance(xat, int) else pl.multiple_of(xat, 16)
                mine = xf[pl.ds(xat, R), :]
                xw = xr[0, pl.ds(xat, R), :].astype(F32)
                xe = xr[1, pl.ds(xat, R), :].astype(F32)
                pair = pl.multiple_of(f.c0 + (v // 2) * 16, 16)
                odd = lax.rem(v, 2) == 1

                def corner(j):
                    ts = [cr[m, j, pl.ds(pair, 16), :].astype(F32) for m in range(NR)]
                    hs = [jnp.where(odd, t[8:16], t[0:8]) for t in ts]
                    return hs[0] if NR == 1 else jnp.where(sub8 < W, hs[0], hs[1])

                mine = jnp.concatenate([mine, corner(1)], axis=0)
                xw = jnp.concatenate([xw, corner(0)], axis=0)
                xe = jnp.concatenate([xe, corner(2)], axis=0)
                qw = jnp.where(low, xw, mine)
                qe = jnp.where(low, mine, xe)
                sums[4] += qw
                sums[5] += qe
            else:
                qw = wt[v] + cc[4] * mean[1]
                qe = et[v] + cc[4] * mean[2]
            p = jnp.where(lax.rem(lane, 8) == W - 1, qw, pltpu.roll(qe, 126, 1))
            if not last:
                uw = stencil(E, qw, pltpu.roll(qw, 1, 1), pltpu.roll(qw, 127, 1), *cc[:4])
                ue = stencil(E, qe, pltpu.roll(qe, 1, 1), pltpu.roll(qe, 127, 1), *cc[:4])
                wt[v] = uw
                et[v] = ue
                sums[1] += uw
                sums[2] += ue
            total = sums[0] if not last else None
            total0 = sums[3] if first else None
            if first:
                at = pl.multiple_of(f.z0 + v * ZG + n * 8, 16)
                lost = zr[NR - 1, pl.ds(at, 16), :].astype(F32)
            for k0 in range(0, n, BT):
                batch = range(k0, k0 + BT)
                qs = []
                for k in batch:
                    l = v * G + k
                    if first:
                        if k % 2 == 0:
                            at = pl.multiple_of(f.z0 + v * ZG + k * 8, 16)
                            ts = [zr[m, pl.ds(at, 16), :].astype(F32) for m in range(NR)]
                            zpair = ts[0] if NR == 1 else jnp.where(lax.rem(sub_iota(16), 8) < W, ts[0], ts[1])
                        edge = zpair[(k % 2) * 8 : (k % 2) * 8 + 8]
                        edge = edge + jnp.where(sub8 == 7, lost[k : k + 1], 0.0)
                        q = jnp.concatenate([own[l], edge], axis=0)
                        total0 = total0 + q
                    else:
                        q = ext[l] + co[3, l] * mean[0]
                    qs.append(q)
                us = []
                for k, q in zip(batch, qs):
                    a, b, c, d, km = scalars(co, v * G + k)
                    h = pltpu.roll(p, (125 - 8 * k) % 128, 1)
                    wv = jnp.where(is0, h, pltpu.roll(q, 1, 1))
                    ev = jnp.where(is127, h, pltpu.roll(q, 127, 1))
                    us.append(stencil(E, q, wv, ev, a, b, c, d))
                for k, u in zip(batch, us):
                    l = v * G + k
                    if last:
                        own[l] = u[0:R]
                    else:
                        ext[l] = u
                        total = total + u
            if not last:
                sums[0] = total
            if first:
                sums[3] = total0
            if after is not None:
                after(v, n)

        f.groups(group)

    def fold(x):
        for s in (8, 16, 32, 64):
            x = x + pltpu.roll(x, s, 1)
        return x

    def v_copy(src, dst, i):
        return pltpu.make_async_remote_copy(
            src_ref=src, dst_ref=dst, send_sem=v_ss.at[i], recv_sem=v_rs.at[i],
            device_id={"vert": other}, device_id_type=MESH,
        )

    def send0(f, sums, kk, vs, vr, i):
        for j in range(6):
            s = sums[j]
            vs[j, 0 : f.E, :] = s if j in (0, 3) else fold(s)
        vs[6, 0:8, :] = jnp.full((8, 128), kk, F32)
        cp = v_copy(vs, vr, i)
        cp.start()
        return cp

    def send1(f, sums, us, ur, slot, i):
        for j in range(3 if slot == 0 else 1):
            us[slot, j] = sums[j] if j == 0 else fold(sums[j])
        if slot == 1:
            cp = v_copy(us.at[slot, 0], ur.at[slot, 0], i)
        else:
            cp = v_copy(us.at[slot], ur.at[slot], i)
        cp.start()
        return cp

    def means0(f, vs, vr):
        inv = F32(1.0 / f.total)
        ksum = (vs[6, 0:1, :] + vr[6, 0:1, :]) * inv
        m0 = [(vs[3 + j] + vr[3 + j]) * inv for j in range(3)]
        m1 = [(vs[j] + vr[j]) * inv + ksum * m0[j] for j in range(3)]
        return m0, m1, ksum

    for side in range(2):
        x_copy(1 - side).wait_recv()
    for n in range(NR):
        for j in range(3):
            c_copy(n, j).wait_recv()

    one_pass(fa, ac, a_cl, a_own, a_ext, a_w, a_e, a_sum, None, first=True)
    a0 = send0(fa, a_sum, a_k, a_vs, a_vr, 0)
    one_pass(fo, oc, o_cl, o_own, o_ext, o_w, o_e, o_sum, None, first=True)
    o0 = send0(fo, o_sum, o_k, o_vs, o_vr, 1)

    def r_wait(k, carry):
        r_copy(k).wait_recv()
        return carry

    lax.fori_loop(1, peers, r_wait, 0)
    loads[2].wait()
    nbo = rem_ref.shape[1]
    subo = sub_iota(nbo)

    def entry(e, acc):
        s = listed(me, e, 0)
        dev = s // nba
        t = lax.rem(listed(me, e, 1), nbo)
        wi = listed(me, e, 2)

        def before(x, got):
            return jnp.where(listed(me, x, 0) // nba == dev, jnp.int32(1), got)

        second = jnp.int32(0)
        if isinstance(e, int):
            for x in range(e):
                second = before(x, second)
        else:
            second = lax.fori_loop(0, e, before, second)
        prod = jnp.dot(rr[dev].astype(BF16), wbuf[wi], preferred_element_type=F32)
        hit = subo == t
        out = []
        for f in range(flux_f):
            row = jnp.where(second == 1, prod[flux_f + f : flux_f + f + 1], prod[f : f + 1])
            out.append(acc[f] + jnp.where(hit, row, 0.0))
        return tuple(out)

    acc = tuple(jnp.zeros((nbo, 128), F32) for _ in range(flux_f))
    if entries <= 16:
        for e in range(entries):
            acc = entry(e, acc)
    else:
        acc = lax.fori_loop(0, entries, entry, acc)
    for f in range(flux_f):
        rem_ref[f] = acc[f]

    def keep(f, sums, ms):
        for j in range(3):
            sums[j] = ms[j]

    a0.wait()
    am0, am1, a_ks = means0(fa, a_vs, a_vr)
    for j in range(3):
        a_vs[j] = am0[j]
        a_vs[3 + j] = am1[j]
    one_pass(fa, ac, a_cl, a_own, a_ext, a_w, a_e, a_sum, a_vs.at[0:3])
    a1 = send1(fa, a_sum, a_us, a_ur, 0, 2)

    o0.wait()
    om0, om1, o_ks = means0(fo, o_vs, o_vr)
    for j in range(3):
        o_vs[j] = om0[j]
        o_vs[3 + j] = om1[j]
    one_pass(fo, oc, o_cl, o_own, o_ext, o_w, o_e, o_sum, o_vs.at[0:3])
    o1 = send1(fo, o_sum, o_us, o_ur, 0, 3)

    one_pass(fa, ac, a_cl, a_own, a_ext, a_w, a_e, a_sum, a_vs.at[3:6])
    a2 = send1(fa, a_sum, a_us, a_ur, 1, 4)
    one_pass(fo, oc, o_cl, o_own, o_ext, o_w, o_e, o_sum, o_vs.at[3:6])
    o2 = send1(fo, o_sum, o_us, o_ur, 1, 5)

    def mean2(f, us, ur, vs, ks):
        inv = F32(1.0 / f.total)
        for j in range(3):
            vs[j] = (us[0, j] + ur[0, j]) * inv + ks * vs[3 + j]

    def out_copies(own, hbm, base):
        def after(v, n):
            at = v * G
            pltpu.make_async_copy(own.at[pl.ds(at, n)], hbm.at[pl.ds(at, n)], out_sem.at[base + v]).start()

        return after

    a1.wait()
    mean2(fa, a_us, a_ur, a_vs, a_ks)
    one_pass(fa, ac, a_cl, a_own, a_ext, a_w, a_e, a_sum, a_vs.at[0:3], last=True, after=out_copies(a_own, ua_hbm, 0))
    o1.wait()
    mean2(fo, o_us, o_ur, o_vs, o_ks)
    one_pass(fo, oc, o_cl, o_own, o_ext, o_w, o_e, o_sum, o_vs.at[0:3], last=True, after=out_copies(o_own, uo_hbm, fa.V))
    a2.wait()
    o2.wait()
    ma_ref[...] = ((a_us[1, 0] + a_ur[1, 0]) * F32(1.0 / fa.total) + a_ks * a_vs[0])[0 : fa.R]
    mo_ref[...] = ((o_us[1, 0] + o_ur[1, 0]) * F32(1.0 / fo.total) + o_ks * o_vs[0])[0 : fo.R]

    for f, own, hbm, base in ((fa, a_own, ua_hbm, 0), (fo, o_own, uo_hbm, fa.V)):
        for v, n in f.chunks:
            at = v * G
            pltpu.make_async_copy(own.at[pl.ds(at, n)], hbm.at[pl.ds(at, n)], out_sem.at[base + v]).wait()
    for side in range(2):
        x_copy(side).wait_send()
    for n in range(NR):
        for j in range(3):
            c_copy(n, j).wait_send()
        for i in range(fa.V):
            z_copy(fa, n, i, 0).wait_send()
        for i in range(fo.V):
            z_copy(fo, n, i, oz).wait_send()

    def r_done(k, carry):
        r_copy(k).wait_send()
        return carry

    lax.fori_loop(1, peers, r_done, 0)


def body(H, C, KV, atm_state, atm_coeffs, ocean_state, ocean_coeffs, atm_flux, remap_weights, remap_list, ocean_mask):
    la, ra, _ = atm_state.shape
    lo, ro, _ = ocean_state.shape
    flux_f, nba, _ = atm_flux.shape
    entries = remap_list.shape[1]
    nbo = ocean_mask.shape[0]
    peers = H * C
    NR = 1 if C == 2 else 2
    remap_list = jnp.transpose(remap_list, (2, 0, 1))
    va, vo = (la + G - 1) // G, (lo + G - 1) // G
    fa = Field(la, ra, KV * la, 0, 0, 0, 0)
    fo = Field(lo, ro, KV * lo, va * ZG, va * ra, rup(va, 2) * 8, 0)
    zrows = (va + vo) * ZG
    xrows = va * ra + vo * ro
    crows = (rup(va, 2) + rup(vo, 2)) * 8
    V = pltpu.VMEM
    DMA = pltpu.SemaphoreType.DMA
    scratch = [
        V((la, ra, 128), F32), V((lo, ro, 128), F32),
        V((la, fa.E, 128), F32), V((lo, fo.E, 128), F32),
        V((va, fa.E, 128), F32), V((va, fa.E, 128), F32),
        V((vo, fo.E, 128), F32), V((vo, fo.E, 128), F32),
        V((va, 8, 128), F32), V((vo, 8, 128), F32),
        V((6, fa.E, 128), F32), V((6, fo.E, 128), F32),
        V(remap_weights.shape, BF16),
        V((zrows, 128), BF16), V((NR, zrows, 128), BF16),
        V((xrows, 128), F32), V((xrows, 128), BF16), V((2, xrows, 128), BF16),
        V((crows, 128), BF16), V((NR, 3, crows, 128), BF16),
        V((7, fa.E, 128), F32), V((7, fa.E, 128), F32),
        V((7, fo.E, 128), F32), V((7, fo.E, 128), F32),
        V((2, 3, fa.E, 128), F32), V((2, 3, fa.E, 128), F32),
        V((2, 3, fo.E, 128), F32), V((2, 3, fo.E, 128), F32),
        V((peers * 8, 128), F32), V((peers, 8, 128), F32), V((peers, 8, 128), F32),
        DMA((3,)), DMA((va + vo,)),
        DMA((NR, va + vo)), DMA((NR, va + vo)),
        DMA((2,)), DMA((2,)),
        DMA((NR, 3)), DMA((NR, 3)),
        DMA((6,)), DMA((6,)),
        DMA((peers,)), DMA((peers,)),
    ]
    anyspec = pl.BlockSpec(memory_space=pl.ANY)
    hbm = pl.BlockSpec(memory_space=pltpu.HBM)
    vspec = pl.BlockSpec(memory_space=pltpu.VMEM)
    sspec = pl.BlockSpec(memory_space=pltpu.SMEM)
    ua, uo, ma, mo, rem = pl.pallas_call(
        functools.partial(kernel, fa, fo, NR, H, C, flux_f, nba, entries),
        out_shape=(
            jax.ShapeDtypeStruct((la, ra, 128), F32),
            jax.ShapeDtypeStruct((lo, ro, 128), F32),
            jax.ShapeDtypeStruct((ra, 128), F32),
            jax.ShapeDtypeStruct((ro, 128), F32),
            jax.ShapeDtypeStruct((flux_f, nbo, 128), F32),
        ),
        in_specs=[hbm, hbm, hbm, vspec, sspec, sspec, sspec],
        out_specs=(anyspec, anyspec, vspec, vspec, vspec),
        scratch_shapes=scratch,
        compiler_params=pltpu.CompilerParams(
            collective_id=0, has_side_effects=True, vmem_limit_bytes=32 * 1024 * 1024
        ),
    )(*[pltpu.with_memory_space_constraint(x, pltpu.HBM) for x in (atm_state, ocean_state, remap_weights)], atm_flux, atm_coeffs, ocean_coeffs, remap_list)
    return (
        ua + atm_coeffs[3][:, None, None] * ma[None],
        uo + ocean_coeffs[3][:, None, None] * mo[None],
        rem * ocean_mask.astype(F32)[None],
    )


def solution(mesh):
    H, C, KV = mesh.shape["horiz"], mesh.shape["comp"], mesh.shape["vert"]
    return jax.shard_map(
        functools.partial(body, H, C, KV),
        mesh=mesh,
        in_specs=(
            P("vert", ("runs", "comp"), "horiz"),
            P(None, "vert"),
            P("vert", ("runs", "comp"), "horiz"),
            P(None, "vert"),
            P("vert", ("runs", "horiz", "comp"), None),
            P(),
            P(),
            P(("horiz", "comp"), None),
        ),
        out_specs=(
            P("vert", ("runs", "comp"), "horiz"),
            P("vert", ("runs", "comp"), "horiz"),
            P("vert", ("runs", "horiz", "comp"), None),
        ),
        check_vma=False,
    )
```

```python
import functools

import jax
import jax.numpy as jnp
from jax import lax
from jax.experimental import pallas as pl
from jax.experimental.pallas import tpu as pltpu
from jax.sharding import PartitionSpec as P

F32 = jnp.float32
BF16 = jnp.bfloat16
W = 4
ZG = 16 * 8 + 16
G = 16


def rup(x, m):
    return (x + m - 1) // m * m


def lane_iota(rows):
    return lax.broadcasted_iota(jnp.int32, (rows, 128), 1)


def sub_iota(rows):
    return lax.broadcasted_iota(jnp.int32, (rows, 128), 0)


BT = 4


class Field:
    def __init__(self, levels, rows, total, z0, x0, c0, s0):
        self.L, self.R, self.total = levels, rows, total
        self.E = rows + 2 * W
        self.V = (levels + G - 1) // G
        self.full = levels // G
        self.tail = levels - self.full * G
        self.z0, self.x0, self.c0, self.s0 = z0, x0, c0, s0
        self.chunks = [(v, min(G, levels - v * G)) for v in range(self.V)]

    def groups(self, fn):
        if self.full:

            def step(v, carry):
                fn(v, G)
                return carry

            lax.fori_loop(0, self.full, step, 0)
        if self.tail:
            fn(self.full, self.tail)


def kernel(
    fa, fo, NR, H, C, flux_f, nba, entries,
    a_hbm, o_hbm, w_hbm, flux_ref, ac, oc, rl,
    ua_hbm, uo_hbm, ma_ref, mo_ref, rem_ref, ka_ref, ko_ref,
    a_own, o_own, a_ext, o_ext, a_w, a_e, o_w, o_e, a_cl, o_cl,
    a_sum, o_sum, wbuf,
    zs, zr, xf, xs, xr, cs, cr,
    a_vs, a_vr, o_vs, o_vr, a_us, a_ur, o_us, o_ur,
    sel, rs, rr,
    ld_sem, out_sem, z_ss, z_rs, x_ss, x_rs, c_ss, c_rs, v_ss, v_rs, r_ss, r_rs,
):
    def listed(p, e, i):
        return rl[i, p, e]

    hi = lax.axis_index("horiz")
    ci = lax.axis_index("comp")
    vi = lax.axis_index("vert")
    peers = H * C
    me = hi * C + ci
    west, east = lax.rem(hi + H - 1, H), lax.rem(hi + 1, H)
    north, south = lax.rem(ci + 1, C), lax.rem(ci + C - 1, C)
    other = 1 - vi
    MESH = pl.DeviceIdType.MESH

    loads = [
        pltpu.make_async_copy(a_hbm, a_own, ld_sem.at[0]),
        pltpu.make_async_copy(o_hbm, o_own, ld_sem.at[1]),
        pltpu.make_async_copy(w_hbm, wbuf, ld_sem.at[2]),
    ]
    for load in loads:
        load.start()

    barrier = pltpu.get_barrier_semaphore()

    def greet(k, carry):
        peer = lax.rem(me + k, peers)
        pl.semaphore_signal(
            barrier, inc=1, device_id={"horiz": peer // C, "comp": lax.rem(peer, C)}, device_id_type=MESH
        )
        return carry

    pl.semaphore_signal(barrier, inc=1, device_id={"vert": other}, device_id_type=MESH)
    lax.fori_loop(1, peers, greet, 0)

    def scalars(co, l):
        cx, cy, kd, km = co[0, l], co[1, l], co[2, l], co[3, l]
        return 1.0 - cx - cy - 4.0 * kd - km, cx + kd, cy + kd, kd, km

    lane1 = lane_iota(1)

    def spread(f, co, cl):
        def group(v, n):
            rows = [jnp.zeros((1, 128), F32) for _ in range(5)]
            for k in range(n):
                here = (lane1 // 8) == k
                rows = [jnp.where(here, s, r) for s, r in zip(scalars(co, v * G + k), rows)]
            for i in range(5):
                cl[v, i : i + 1, :] = rows[i]

        f.groups(group)

    spread(fa, ac, a_cl)
    spread(fo, oc, o_cl)

    def total_km(f, co, kept):
        def add(l, s):
            kept[0, l] = co[3, l]
            return s + co[3, l]

        return lax.fori_loop(0, f.L, add, jnp.float32(0))

    a_k = total_km(fa, ac, ka_ref)
    o_k = total_km(fo, oc, ko_ref)

    sub8 = sub_iota(8)
    sub16 = sub_iota(16)

    def pack(f, own):
        lane = lane_iota(f.R)

        def group(v, n):
            acc = jnp.zeros((f.R, 128), F32)
            z_prev = None
            lost = jnp.zeros((16, 128), F32)
            for k in range(n):
                q = own[v * G + k]
                acc = jnp.where((lane // 8) == k, pltpu.roll(q, (8 * k + 4) % 128, 1), acc)
                z = jnp.where(sub8 < W, q[0:8], q[f.R - 8 : f.R])
                top = q[f.R - 1 : f.R]
                lost = jnp.where(sub16 == k, top - top.astype(BF16).astype(F32), lost)
                if k % 2 == 0:
                    z_prev = z
                else:
                    at = pl.multiple_of(f.z0 + v * ZG + (k - 1) * 8, 16)
                    zs[pl.ds(at, 16), :] = jnp.concatenate([z_prev, z], axis=0).astype(BF16)
            at = pl.multiple_of(f.z0 + v * ZG + n * 8, 16)
            zs[pl.ds(at, 16), :] = lost.astype(BF16)
            at = pl.multiple_of(f.x0 + v * f.R, 16)
            xf[pl.ds(at, f.R), :] = acc
            xs[pl.ds(at, f.R), :] = acc.astype(BF16)

        f.groups(group)
        for v in range(0, rup(f.V, 2), 2):
            parts = []
            for u in (v, v + 1):
                if u < f.V:
                    base = f.x0 + u * f.R
                    parts.append(
                        jnp.where(sub8 < W, xf[base : base + 8, :], xf[base + f.R - 8 : base + f.R, :])
                    )
                else:
                    parts.append(jnp.zeros((8, 128), F32))
            at = f.c0 + v * 8
            cs[at : at + 16, :] = jnp.concatenate(parts, axis=0).astype(BF16)

    row_nbrs = [north] if NR == 1 else [north, south]

    def slot_at(n):
        return n if NR == 1 else 1 - n

    def z_copy(f, n, i, base):
        v, cnt = f.chunks[i]
        at, size = f.z0 + v * ZG, cnt * 8 + 16
        return pltpu.make_async_remote_copy(
            src_ref=zs.at[pl.ds(at, size)],
            dst_ref=zr.at[slot_at(n), pl.ds(at, size)],
            send_sem=z_ss.at[n, base + i],
            recv_sem=z_rs.at[slot_at(n), base + i],
            device_id={"comp": row_nbrs[n]},
            device_id_type=MESH,
        )

    def x_copy(side):
        return pltpu.make_async_remote_copy(
            src_ref=xs,
            dst_ref=xr.at[1 - side],
            send_sem=x_ss.at[side],
            recv_sem=x_rs.at[1 - side],
            device_id={"horiz": west if side == 0 else east},
            device_id_type=MESH,
        )

    def c_copy(n, j):
        col = (west, hi, east)[j]
        return pltpu.make_async_remote_copy(
            src_ref=cs,
            dst_ref=cr.at[slot_at(n), 2 - j],
            send_sem=c_ss.at[n, j],
            recv_sem=c_rs.at[slot_at(n), 2 - j],
            device_id={"horiz": col, "comp": row_nbrs[n]},
            device_id_type=MESH,
        )

    oz = fa.V
    loads[0].wait()
    pack(fa, a_own)
    pl.semaphore_wait(barrier, peers)
    for i in range(fa.V):
        for n in range(NR):
            z_copy(fa, n, i, 0).start()
    loads[1].wait()
    pack(fo, o_own)
    for side in range(2):
        x_copy(side).start()
    for n in range(NR):
        for j in range(3):
            c_copy(n, j).start()
    for i in range(fo.V):
        for n in range(NR):
            z_copy(fo, n, i, oz).start()

    lane8 = lane_iota(8)

    def choose(p, carry):
        first, last = jnp.int32(0), jnp.int32(0)
        seen = jnp.int32(0)

        def look(e, st):
            first, last, seen = st
            s = listed(p, e, 0)
            here = (s // nba) == me
            b = lax.rem(s, nba)
            first = jnp.where(jnp.logical_and(here, seen == 0), b, first)
            last = jnp.where(here, b, last)
            seen = jnp.where(here, 1, seen)
            return first, last, seen

        if entries <= 16:
            st = (first, last, seen)
            for e in range(entries):
                st = look(e, st)
        else:
            st = lax.fori_loop(0, entries, look, (first, last, seen))
        first, last, _ = st
        want = jnp.where(sub8 < flux_f, first, last) + lax.rem(sub8, flux_f) * nba
        at = pl.multiple_of(p * 8, 8)
        sel[pl.ds(at, 8), :] = jnp.where(lane8 == want, 1.0, 0.0)
        return carry

    lax.fori_loop(0, peers, choose, 0)
    depth = flux_f * nba
    picked = jnp.dot(
        sel[:, 0:depth].astype(BF16),
        flux_ref[...].reshape(depth, 128),
        preferred_element_type=F32,
    )
    rs[...] = picked.reshape(peers, 8, 128)
    rr[me] = rs[me]

    def r_copy(k):
        peer = lax.rem(me + k, peers)
        return pltpu.make_async_remote_copy(
            src_ref=rs.at[peer],
            dst_ref=rr.at[me],
            send_sem=r_ss.at[k],
            recv_sem=r_rs.at[k],
            device_id={"horiz": peer // C, "comp": lax.rem(peer, C)},
            device_id_type=MESH,
        )

    def r_start(k, carry):
        r_copy(k).start()
        return carry

    lax.fori_loop(1, peers, r_start, 0)

    def stencil(E, q, wv, ev, a, b, c, d):
        return a * q + b * wv + c * pltpu.roll(q, 1, 0) + d * (ev + pltpu.roll(q, E - 1, 0))

    def one_pass(f, co, cl, own, ext, wt, et, sums, mean, first=False, last=False, after=None):
        E, R = f.E, f.R
        lane = lane_iota(E)
        low = lax.rem(lane, 8) < W
        is0, is127 = lane == 0, lane == 127
        oz_f = 0 if f is fa else fa.V
        nsum = 6 if first else 3
        if not last:
            sums[...] = jnp.zeros_like(sums)

        def rows_of(ref, idx, at):
            t = ref[idx + (pl.ds(pl.multiple_of(at - lax.rem(at, 16), 16), 16), slice(None))].astype(F32)
            return t

        def group(v, n):
            cc = [cl[v, i : i + 1, :] for i in range(5)]
            if first:
                for m in range(NR):
                    size = n * 8 + 16
                    at = f.z0 + v * ZG
                    at = at if isinstance(at, int) else pl.multiple_of(at, 16)
                    pltpu.make_async_remote_copy(
                        src_ref=zs.at[pl.ds(at, size)],
                        dst_ref=zr.at[m, pl.ds(at, size)],
                        send_sem=z_ss.at[m, oz_f + v],
                        recv_sem=z_rs.at[m, oz_f + v],
                        device_id={"comp": row_nbrs[m]},
                        device_id_type=MESH,
                    ).wait_recv()
                xat = f.x0 + v * R
                xat = xat if isinstance(xat, int) else pl.multiple_of(xat, 16)
                mine = xf[pl.ds(xat, R), :]
                xw = xr[0, pl.ds(xat, R), :].astype(F32)
                xe = xr[1, pl.ds(xat, R), :].astype(F32)
                pair = pl.multiple_of(f.c0 + (v // 2) * 16, 16)
                odd = lax.rem(v, 2) == 1

                def corner(j):
                    ts = [cr[m, j, pl.ds(pair, 16), :].astype(F32) for m in range(NR)]
                    hs = [jnp.where(odd, t[8:16], t[0:8]) for t in ts]
                    return hs[0] if NR == 1 else jnp.where(sub8 < W, hs[0], hs[1])

                mine = jnp.concatenate([mine, corner(1)], axis=0)
                xw = jnp.concatenate([xw, corner(0)], axis=0)
                xe = jnp.concatenate([xe, corner(2)], axis=0)
                qw = jnp.where(low, xw, mine)
                qe = jnp.where(low, mine, xe)
                sums[4] += qw
                sums[5] += qe
            else:
                qw = wt[v] + cc[4] * mean[1]
                qe = et[v] + cc[4] * mean[2]
            p = jnp.where(lax.rem(lane, 8) == W - 1, qw, pltpu.roll(qe, 126, 1))
            if not last:
                uw = stencil(E, qw, pltpu.roll(qw, 1, 1), pltpu.roll(qw, 127, 1), *cc[:4])
                ue = stencil(E, qe, pltpu.roll(qe, 1, 1), pltpu.roll(qe, 127, 1), *cc[:4])
                wt[v] = uw
                et[v] = ue
                sums[1] += uw
                sums[2] += ue
            total = sums[0] if not last else None
            total0 = sums[3] if first else None
            if first:
                at = pl.multiple_of(f.z0 + v * ZG + n * 8, 16)
                lost = zr[NR - 1, pl.ds(at, 16), :].astype(F32)
            for k0 in range(0, n, BT):
                batch = range(k0, k0 + BT)
                qs = []
                for k in batch:
                    l = v * G + k
                    if first:
                        if k % 2 == 0:
                            at = pl.multiple_of(f.z0 + v * ZG + k * 8, 16)
                            ts = [zr[m, pl.ds(at, 16), :].astype(F32) for m in range(NR)]
                            zpair = ts[0] if NR == 1 else jnp.where(lax.rem(sub_iota(16), 8) < W, ts[0], ts[1])
                        edge = zpair[(k % 2) * 8 : (k % 2) * 8 + 8]
                        edge = edge + jnp.where(sub8 == 7, lost[k : k + 1], 0.0)
                        q = jnp.concatenate([own[l], edge], axis=0)
                        total0 = total0 + q
                    else:
                        q = ext[l] + co[3, l] * mean[0]
                    qs.append(q)
                us = []
                for k, q in zip(batch, qs):
                    a, b, c, d, km = scalars(co, v * G + k)
                    h = pltpu.roll(p, (125 - 8 * k) % 128, 1)
                    wv = jnp.where(is0, h, pltpu.roll(q, 1, 1))
                    ev = jnp.where(is127, h, pltpu.roll(q, 127, 1))
                    us.append(stencil(E, q, wv, ev, a, b, c, d))
                for k, u in zip(batch, us):
                    l = v * G + k
                    if last:
                        own[l] = u[0:R]
                    else:
                        ext[l] = u
                        total = total + u
            if not last:
                sums[0] = total
            if first:
                sums[3] = total0
            if after is not None:
                after(v, n)

        f.groups(group)

    def fold(x):
        for s in (8, 16, 32, 64):
            x = x + pltpu.roll(x, s, 1)
        return x

    def v_copy(src, dst, i):
        return pltpu.make_async_remote_copy(
            src_ref=src, dst_ref=dst, send_sem=v_ss.at[i], recv_sem=v_rs.at[i],
            device_id={"vert": other}, device_id_type=MESH,
        )

    def send0(f, sums, kk, vs, vr, i):
        for j in range(6):
            s = sums[j]
            vs[j, 0 : f.E, :] = s if j in (0, 3) else fold(s)
        vs[6, 0:8, :] = jnp.full((8, 128), kk, F32)
        cp = v_copy(vs, vr, i)
        cp.start()
        return cp

    def send1(f, sums, us, ur, slot, i):
        for j in range(3 if slot == 0 else 1):
            us[slot, j] = sums[j] if j == 0 else fold(sums[j])
        if slot == 1:
            cp = v_copy(us.at[slot, 0], ur.at[slot, 0], i)
        else:
            cp = v_copy(us.at[slot], ur.at[slot], i)
        cp.start()
        return cp

    def means0(f, vs, vr):
        inv = F32(1.0 / f.total)
        ksum = (vs[6, 0:1, :] + vr[6, 0:1, :]) * inv
        m0 = [(vs[3 + j] + vr[3 + j]) * inv for j in range(3)]
        m1 = [(vs[j] + vr[j]) * inv + ksum * m0[j] for j in range(3)]
        return m0, m1, ksum

    for side in range(2):
        x_copy(1 - side).wait_recv()
    for n in range(NR):
        for j in range(3):
            c_copy(n, j).wait_recv()

    one_pass(fa, ac, a_cl, a_own, a_ext, a_w, a_e, a_sum, None, first=True)
    a0 = send0(fa, a_sum, a_k, a_vs, a_vr, 0)
    one_pass(fo, oc, o_cl, o_own, o_ext, o_w, o_e, o_sum, None, first=True)
    o0 = send0(fo, o_sum, o_k, o_vs, o_vr, 1)

    def r_wait(k, carry):
        r_copy(k).wait_recv()
        return carry

    lax.fori_loop(1, peers, r_wait, 0)
    loads[2].wait()
    nbo = rem_ref.shape[1]
    subo = sub_iota(nbo)

    def entry(e, acc):
        s = listed(me, e, 0)
        dev = s // nba
        t = lax.rem(listed(me, e, 1), nbo)
        wi = listed(me, e, 2)

        def before(x, got):
            return jnp.where(listed(me, x, 0) // nba == dev, jnp.int32(1), got)

        second = jnp.int32(0)
        if isinstance(e, int):
            for x in range(e):
                second = before(x, second)
        else:
            second = lax.fori_loop(0, e, before, second)
        prod = jnp.dot(rr[dev].astype(BF16), wbuf[wi], preferred_element_type=F32)
        hit = subo == t
        out = []
        for f in range(flux_f):
            row = jnp.where(second == 1, prod[flux_f + f : flux_f + f + 1], prod[f : f + 1])
            out.append(acc[f] + jnp.where(hit, row, 0.0))
        return tuple(out)

    acc = tuple(jnp.zeros((nbo, 128), F32) for _ in range(flux_f))
    if entries <= 16:
        for e in range(entries):
            acc = entry(e, acc)
    else:
        acc = lax.fori_loop(0, entries, entry, acc)
    for f in range(flux_f):
        rem_ref[f] = acc[f]

    def keep(f, sums, ms):
        for j in range(3):
            sums[j] = ms[j]

    a0.wait()
    am0, am1, a_ks = means0(fa, a_vs, a_vr)
    for j in range(3):
        a_vs[j] = am0[j]
        a_vs[3 + j] = am1[j]
    one_pass(fa, ac, a_cl, a_own, a_ext, a_w, a_e, a_sum, a_vs.at[0:3])
    a1 = send1(fa, a_sum, a_us, a_ur, 0, 2)

    o0.wait()
    om0, om1, o_ks = means0(fo, o_vs, o_vr)
    for j in range(3):
        o_vs[j] = om0[j]
        o_vs[3 + j] = om1[j]
    one_pass(fo, oc, o_cl, o_own, o_ext, o_w, o_e, o_sum, o_vs.at[0:3])
    o1 = send1(fo, o_sum, o_us, o_ur, 0, 3)

    one_pass(fa, ac, a_cl, a_own, a_ext, a_w, a_e, a_sum, a_vs.at[3:6])
    a2 = send1(fa, a_sum, a_us, a_ur, 1, 4)
    one_pass(fo, oc, o_cl, o_own, o_ext, o_w, o_e, o_sum, o_vs.at[3:6])
    o2 = send1(fo, o_sum, o_us, o_ur, 1, 5)

    def mean2(f, us, ur, vs, ks):
        inv = F32(1.0 / f.total)
        for j in range(3):
            vs[j] = (us[0, j] + ur[0, j]) * inv + ks * vs[3 + j]

    def out_copies(own, hbm, base):
        def after(v, n):
            at = v * G
            pltpu.make_async_copy(own.at[pl.ds(at, n)], hbm.at[pl.ds(at, n)], out_sem.at[base + v]).start()

        return after

    a1.wait()
    mean2(fa, a_us, a_ur, a_vs, a_ks)
    one_pass(fa, ac, a_cl, a_own, a_ext, a_w, a_e, a_sum, a_vs.at[0:3], last=True, after=out_copies(a_own, ua_hbm, 0))
    o1.wait()
    mean2(fo, o_us, o_ur, o_vs, o_ks)
    one_pass(fo, oc, o_cl, o_own, o_ext, o_w, o_e, o_sum, o_vs.at[0:3], last=True, after=out_copies(o_own, uo_hbm, fa.V))
    a2.wait()
    o2.wait()
    ma_ref[...] = ((a_us[1, 0] + a_ur[1, 0]) * F32(1.0 / fa.total) + a_ks * a_vs[0])[0 : fa.R]
    mo_ref[...] = ((o_us[1, 0] + o_ur[1, 0]) * F32(1.0 / fo.total) + o_ks * o_vs[0])[0 : fo.R]

    for f, own, hbm, base in ((fa, a_own, ua_hbm, 0), (fo, o_own, uo_hbm, fa.V)):
        for v, n in f.chunks:
            at = v * G
            pltpu.make_async_copy(own.at[pl.ds(at, n)], hbm.at[pl.ds(at, n)], out_sem.at[base + v]).wait()
    for side in range(2):
        x_copy(side).wait_send()
    for n in range(NR):
        for j in range(3):
            c_copy(n, j).wait_send()
        for i in range(fa.V):
            z_copy(fa, n, i, 0).wait_send()
        for i in range(fo.V):
            z_copy(fo, n, i, oz).wait_send()

    def r_done(k, carry):
        r_copy(k).wait_send()
        return carry

    lax.fori_loop(1, peers, r_done, 0)


def body(H, C, KV, atm_state, atm_coeffs, ocean_state, ocean_coeffs, atm_flux, remap_weights, remap_list, ocean_mask):
    la, ra, _ = atm_state.shape
    lo, ro, _ = ocean_state.shape
    flux_f, nba, _ = atm_flux.shape
    entries = remap_list.shape[1]
    nbo = ocean_mask.shape[0]
    peers = H * C
    NR = 1 if C == 2 else 2
    remap_list = jnp.transpose(remap_list, (2, 0, 1))
    va, vo = (la + G - 1) // G, (lo + G - 1) // G
    fa = Field(la, ra, KV * la, 0, 0, 0, 0)
    fo = Field(lo, ro, KV * lo, va * ZG, va * ra, rup(va, 2) * 8, 0)
    zrows = (va + vo) * ZG
    xrows = va * ra + vo * ro
    crows = (rup(va, 2) + rup(vo, 2)) * 8
    V = pltpu.VMEM
    DMA = pltpu.SemaphoreType.DMA
    scratch = [
        V((la, ra, 128), F32), V((lo, ro, 128), F32),
        V((la, fa.E, 128), F32), V((lo, fo.E, 128), F32),
        V((va, fa.E, 128), F32), V((va, fa.E, 128), F32),
        V((vo, fo.E, 128), F32), V((vo, fo.E, 128), F32),
        V((va, 8, 128), F32), V((vo, 8, 128), F32),
        V((6, fa.E, 128), F32), V((6, fo.E, 128), F32),
        V(remap_weights.shape, BF16),
        V((zrows, 128), BF16), V((NR, zrows, 128), BF16),
        V((xrows, 128), F32), V((xrows, 128), BF16), V((2, xrows, 128), BF16),
        V((crows, 128), BF16), V((NR, 3, crows, 128), BF16),
        V((7, fa.E, 128), F32), V((7, fa.E, 128), F32),
        V((7, fo.E, 128), F32), V((7, fo.E, 128), F32),
        V((2, 3, fa.E, 128), F32), V((2, 3, fa.E, 128), F32),
        V((2, 3, fo.E, 128), F32), V((2, 3, fo.E, 128), F32),
        V((peers * 8, 128), F32), V((peers, 8, 128), F32), V((peers, 8, 128), F32),
        DMA((3,)), DMA((va + vo,)),
        DMA((NR, va + vo)), DMA((NR, va + vo)),
        DMA((2,)), DMA((2,)),
        DMA((NR, 3)), DMA((NR, 3)),
        DMA((6,)), DMA((6,)),
        DMA((peers,)), DMA((peers,)),
    ]
    anyspec = pl.BlockSpec(memory_space=pl.ANY)
    hbm = pl.BlockSpec(memory_space=pltpu.HBM)
    vspec = pl.BlockSpec(memory_space=pltpu.VMEM)
    sspec = pl.BlockSpec(memory_space=pltpu.SMEM)
    ua, uo, ma, mo, rem, ka, ko = pl.pallas_call(
        functools.partial(kernel, fa, fo, NR, H, C, flux_f, nba, entries),
        out_shape=(
            jax.ShapeDtypeStruct((la, ra, 128), F32),
            jax.ShapeDtypeStruct((lo, ro, 128), F32),
            jax.ShapeDtypeStruct((ra, 128), F32),
            jax.ShapeDtypeStruct((ro, 128), F32),
            jax.ShapeDtypeStruct((flux_f, nbo, 128), F32),
            jax.ShapeDtypeStruct((1, la), F32),
            jax.ShapeDtypeStruct((1, lo), F32),
        ),
        in_specs=[hbm, hbm, hbm, vspec, sspec, sspec, sspec],
        out_specs=(anyspec, anyspec, vspec, vspec, vspec, sspec, sspec),
        scratch_shapes=scratch,
        compiler_params=pltpu.CompilerParams(
            collective_id=0, has_side_effects=True, vmem_limit_bytes=32 * 1024 * 1024
        ),
    )(
        *[
            pltpu.with_memory_space_constraint(x, pltpu.HBM)
            for x in (
                atm_state, ocean_state, remap_weights, atm_flux, atm_coeffs, ocean_coeffs, remap_list
            )
        ]
    )
    return (
        ua + ka[0][:, None, None] * ma[None],
        uo + ko[0][:, None, None] * mo[None],
        rem * ocean_mask.astype(F32)[None],
    )


def solution(mesh):
    H, C, KV = mesh.shape["horiz"], mesh.shape["comp"], mesh.shape["vert"]
    return jax.shard_map(
        functools.partial(body, H, C, KV),
        mesh=mesh,
        in_specs=(
            P("vert", ("runs", "comp"), "horiz"),
            P(None, "vert"),
            P("vert", ("runs", "comp"), "horiz"),
            P(None, "vert"),
            P("vert", ("runs", "horiz", "comp"), None),
            P(),
            P(),
            P(("horiz", "comp"), None),
        ),
        out_specs=(
            P("vert", ("runs", "comp"), "horiz"),
            P("vert", ("runs", "comp"), "horiz"),
            P("vert", ("runs", "horiz", "comp"), None),
        ),
        check_vma=False,
    )
```

```python
import functools

import jax
import jax.numpy as jnp
from jax import lax
from jax.experimental import pallas as pl
from jax.experimental.pallas import tpu as pltpu
from jax.sharding import PartitionSpec as P

F32 = jnp.float32
BF16 = jnp.bfloat16
W = 4
ZG = 16 * 8 + 16
G = 16


def rup(x, m):
    return (x + m - 1) // m * m


def lane_iota(rows):
    return lax.broadcasted_iota(jnp.int32, (rows, 128), 1)


def sub_iota(rows):
    return lax.broadcasted_iota(jnp.int32, (rows, 128), 0)


BT = 8


class Field:
    def __init__(self, levels, rows, total, z0, x0, c0, s0):
        self.L, self.R, self.total = levels, rows, total
        self.E = rows + 2 * W
        self.V = (levels + G - 1) // G
        self.full = levels // G
        self.tail = levels - self.full * G
        self.z0, self.x0, self.c0, self.s0 = z0, x0, c0, s0
        self.chunks = [(v, min(G, levels - v * G)) for v in range(self.V)]

    def groups(self, fn):
        if self.full:

            def step(v, carry):
                fn(v, G)
                return carry

            lax.fori_loop(0, self.full, step, 0)
        if self.tail:
            fn(self.full, self.tail)


def kernel(
    fa, fo, NR, H, C, flux_f, nba, entries,
    a_hbm, o_hbm, w_hbm, flux_ref, ac, oc, rl,
    ua_hbm, uo_hbm, ma_ref, mo_ref, rem_ref, ka_ref, ko_ref,
    a_own, o_own, a_ext, o_ext, a_w, a_e, o_w, o_e, a_cl, o_cl,
    a_sum, o_sum, wbuf,
    zs, zr, xf, xs, xr, cs, cr,
    a_vs, a_vr, o_vs, o_vr, a_us, a_ur, o_us, o_ur,
    sel, rs, rr,
    ld_sem, out_sem, z_ss, z_rs, x_ss, x_rs, c_ss, c_rs, v_ss, v_rs, r_ss, r_rs,
):
    def listed(p, e, i):
        return rl[i, p, e]

    hi = lax.axis_index("horiz")
    ci = lax.axis_index("comp")
    vi = lax.axis_index("vert")
    peers = H * C
    me = hi * C + ci
    west, east = lax.rem(hi + H - 1, H), lax.rem(hi + 1, H)
    north, south = lax.rem(ci + 1, C), lax.rem(ci + C - 1, C)
    other = 1 - vi
    MESH = pl.DeviceIdType.MESH

    loads = [
        pltpu.make_async_copy(a_hbm, a_own, ld_sem.at[0]),
        pltpu.make_async_copy(o_hbm, o_own, ld_sem.at[1]),
        pltpu.make_async_copy(w_hbm, wbuf, ld_sem.at[2]),
    ]
    for load in loads:
        load.start()

    barrier = pltpu.get_barrier_semaphore()

    def greet(k, carry):
        peer = lax.rem(me + k, peers)
        pl.semaphore_signal(
            barrier, inc=1, device_id={"horiz": peer // C, "comp": lax.rem(peer, C)}, device_id_type=MESH
        )
        return carry

    pl.semaphore_signal(barrier, inc=1, device_id={"vert": other}, device_id_type=MESH)
    lax.fori_loop(1, peers, greet, 0)

    def scalars(co, l):
        cx, cy, kd, km = co[0, l], co[1, l], co[2, l], co[3, l]
        return 1.0 - cx - cy - 4.0 * kd - km, cx + kd, cy + kd, kd, km

    lane1 = lane_iota(1)

    def spread(f, co, cl):
        def group(v, n):
            rows = [jnp.zeros((1, 128), F32) for _ in range(5)]
            for k in range(n):
                here = (lane1 // 8) == k
                rows = [jnp.where(here, s, r) for s, r in zip(scalars(co, v * G + k), rows)]
            for i in range(5):
                cl[v, i : i + 1, :] = rows[i]

        f.groups(group)

    spread(fa, ac, a_cl)
    spread(fo, oc, o_cl)

    def total_km(f, co, kept):
        def add(l, s):
            kept[0, l] = co[3, l]
            return s + co[3, l]

        return lax.fori_loop(0, f.L, add, jnp.float32(0))

    a_k = total_km(fa, ac, ka_ref)
    o_k = total_km(fo, oc, ko_ref)

    sub8 = sub_iota(8)
    sub16 = sub_iota(16)

    def pack(f, own):
        lane = lane_iota(f.R)

        def group(v, n):
            acc = jnp.zeros((f.R, 128), F32)
            z_prev = None
            lost = jnp.zeros((16, 128), F32)
            for k in range(n):
                q = own[v * G + k]
                acc = jnp.where((lane // 8) == k, pltpu.roll(q, (8 * k + 4) % 128, 1), acc)
                z = jnp.where(sub8 < W, q[0:8], q[f.R - 8 : f.R])
                top = q[f.R - 1 : f.R]
                lost = jnp.where(sub16 == k, top - top.astype(BF16).astype(F32), lost)
                if k % 2 == 0:
                    z_prev = z
                else:
                    at = pl.multiple_of(f.z0 + v * ZG + (k - 1) * 8, 16)
                    zs[pl.ds(at, 16), :] = jnp.concatenate([z_prev, z], axis=0).astype(BF16)
            at = pl.multiple_of(f.z0 + v * ZG + n * 8, 16)
            zs[pl.ds(at, 16), :] = lost.astype(BF16)
            at = pl.multiple_of(f.x0 + v * f.R, 16)
            xf[pl.ds(at, f.R), :] = acc
            xs[pl.ds(at, f.R), :] = acc.astype(BF16)

        f.groups(group)
        for v in range(0, rup(f.V, 2), 2):
            parts = []
            for u in (v, v + 1):
                if u < f.V:
                    base = f.x0 + u * f.R
                    parts.append(
                        jnp.where(sub8 < W, xf[base : base + 8, :], xf[base + f.R - 8 : base + f.R, :])
                    )
                else:
                    parts.append(jnp.zeros((8, 128), F32))
            at = f.c0 + v * 8
            cs[at : at + 16, :] = jnp.concatenate(parts, axis=0).astype(BF16)

    row_nbrs = [north] if NR == 1 else [north, south]

    def slot_at(n):
        return n if NR == 1 else 1 - n

    def z_copy(f, n, i, base):
        v, cnt = f.chunks[i]
        at, size = f.z0 + v * ZG, cnt * 8 + 16
        return pltpu.make_async_remote_copy(
            src_ref=zs.at[pl.ds(at, size)],
            dst_ref=zr.at[slot_at(n), pl.ds(at, size)],
            send_sem=z_ss.at[n, base + i],
            recv_sem=z_rs.at[slot_at(n), base + i],
            device_id={"comp": row_nbrs[n]},
            device_id_type=MESH,
        )

    def x_copy(side):
        return pltpu.make_async_remote_copy(
            src_ref=xs,
            dst_ref=xr.at[1 - side],
            send_sem=x_ss.at[side],
            recv_sem=x_rs.at[1 - side],
            device_id={"horiz": west if side == 0 else east},
            device_id_type=MESH,
        )

    def c_copy(n, j):
        col = (west, hi, east)[j]
        return pltpu.make_async_remote_copy(
            src_ref=cs,
            dst_ref=cr.at[slot_at(n), 2 - j],
            send_sem=c_ss.at[n, j],
            recv_sem=c_rs.at[slot_at(n), 2 - j],
            device_id={"horiz": col, "comp": row_nbrs[n]},
            device_id_type=MESH,
        )

    oz = fa.V
    loads[0].wait()
    pack(fa, a_own)
    loads[1].wait()
    pack(fo, o_own)
    pl.semaphore_wait(barrier, peers)
    for side in range(2):
        x_copy(side).start()
    for n in range(NR):
        for j in range(3):
            c_copy(n, j).start()
    for i in range(fa.V):
        for n in range(NR):
            z_copy(fa, n, i, 0).start()
    for i in range(fo.V):
        for n in range(NR):
            z_copy(fo, n, i, oz).start()

    lane8 = lane_iota(8)

    def choose(p, carry):
        first, last = jnp.int32(0), jnp.int32(0)
        seen = jnp.int32(0)

        def look(e, st):
            first, last, seen = st
            s = listed(p, e, 0)
            here = (s // nba) == me
            b = lax.rem(s, nba)
            first = jnp.where(jnp.logical_and(here, seen == 0), b, first)
            last = jnp.where(here, b, last)
            seen = jnp.where(here, 1, seen)
            return first, last, seen

        if entries <= 16:
            st = (first, last, seen)
            for e in range(entries):
                st = look(e, st)
        else:
            st = lax.fori_loop(0, entries, look, (first, last, seen))
        first, last, _ = st
        want = jnp.where(sub8 < flux_f, first, last) + lax.rem(sub8, flux_f) * nba
        at = pl.multiple_of(p * 8, 8)
        sel[pl.ds(at, 8), :] = jnp.where(lane8 == want, 1.0, 0.0)
        return carry

    lax.fori_loop(0, peers, choose, 0)
    depth = flux_f * nba
    picked = jnp.dot(
        sel[:, 0:depth].astype(BF16),
        flux_ref[...].reshape(depth, 128),
        preferred_element_type=F32,
    )
    rs[...] = picked.reshape(peers, 8, 128)
    rr[me] = rs[me]

    def r_copy(k):
        peer = lax.rem(me + k, peers)
        return pltpu.make_async_remote_copy(
            src_ref=rs.at[peer],
            dst_ref=rr.at[me],
            send_sem=r_ss.at[k],
            recv_sem=r_rs.at[k],
            device_id={"horiz": peer // C, "comp": lax.rem(peer, C)},
            device_id_type=MESH,
        )

    def r_start(k, carry):
        r_copy(k).start()
        return carry

    lax.fori_loop(1, peers, r_start, 0)

    def stencil(E, q, wv, ev, a, b, c, d):
        return a * q + b * wv + c * pltpu.roll(q, 1, 0) + d * (ev + pltpu.roll(q, E - 1, 0))

    def one_pass(f, co, cl, own, ext, wt, et, sums, mean, first=False, last=False, after=None):
        E, R = f.E, f.R
        lane = lane_iota(E)
        low = lax.rem(lane, 8) < W
        is0, is127 = lane == 0, lane == 127
        oz_f = 0 if f is fa else fa.V
        nsum = 6 if first else 3
        if not last:
            sums[...] = jnp.zeros_like(sums)

        def rows_of(ref, idx, at):
            t = ref[idx + (pl.ds(pl.multiple_of(at - lax.rem(at, 16), 16), 16), slice(None))].astype(F32)
            return t

        def group(v, n):
            cc = [cl[v, i : i + 1, :] for i in range(5)]
            if first:
                for m in range(NR):
                    size = n * 8 + 16
                    at = f.z0 + v * ZG
                    at = at if isinstance(at, int) else pl.multiple_of(at, 16)
                    pltpu.make_async_remote_copy(
                        src_ref=zs.at[pl.ds(at, size)],
                        dst_ref=zr.at[m, pl.ds(at, size)],
                        send_sem=z_ss.at[m, oz_f + v],
                        recv_sem=z_rs.at[m, oz_f + v],
                        device_id={"comp": row_nbrs[m]},
                        device_id_type=MESH,
                    ).wait_recv()
                xat = f.x0 + v * R
                xat = xat if isinstance(xat, int) else pl.multiple_of(xat, 16)
                mine = xf[pl.ds(xat, R), :]
                xw = xr[0, pl.ds(xat, R), :].astype(F32)
                xe = xr[1, pl.ds(xat, R), :].astype(F32)
                pair = pl.multiple_of(f.c0 + (v // 2) * 16, 16)
                odd = lax.rem(v, 2) == 1

                def corner(j):
                    ts = [cr[m, j, pl.ds(pair, 16), :].astype(F32) for m in range(NR)]
                    hs = [jnp.where(odd, t[8:16], t[0:8]) for t in ts]
                    return hs[0] if NR == 1 else jnp.where(sub8 < W, hs[0], hs[1])

                mine = jnp.concatenate([mine, corner(1)], axis=0)
                xw = jnp.concatenate([xw, corner(0)], axis=0)
                xe = jnp.concatenate([xe, corner(2)], axis=0)
                qw = jnp.where(low, xw, mine)
                qe = jnp.where(low, mine, xe)
                sums[4] += qw
                sums[5] += qe
            else:
                qw = wt[v] + cc[4] * mean[1]
                qe = et[v] + cc[4] * mean[2]
            p = jnp.where(lax.rem(lane, 8) == W - 1, qw, pltpu.roll(qe, 126, 1))
            if not last:
                uw = stencil(E, qw, pltpu.roll(qw, 1, 1), pltpu.roll(qw, 127, 1), *cc[:4])
                ue = stencil(E, qe, pltpu.roll(qe, 1, 1), pltpu.roll(qe, 127, 1), *cc[:4])
                wt[v] = uw
                et[v] = ue
                sums[1] += uw
                sums[2] += ue
            total = sums[0] if not last else None
            total0 = sums[3] if first else None
            if first:
                at = pl.multiple_of(f.z0 + v * ZG + n * 8, 16)
                lost = zr[NR - 1, pl.ds(at, 16), :].astype(F32)
            for k0 in range(0, n, BT):
                batch = range(k0, k0 + BT)
                qs = []
                for k in batch:
                    l = v * G + k
                    if first:
                        if k % 2 == 0:
                            at = pl.multiple_of(f.z0 + v * ZG + k * 8, 16)
                            ts = [zr[m, pl.ds(at, 16), :].astype(F32) for m in range(NR)]
                            zpair = ts[0] if NR == 1 else jnp.where(lax.rem(sub_iota(16), 8) < W, ts[0], ts[1])
                        edge = zpair[(k % 2) * 8 : (k % 2) * 8 + 8]
                        edge = edge + jnp.where(sub8 == 7, lost[k : k + 1], 0.0)
                        q = jnp.concatenate([own[l], edge], axis=0)
                        total0 = total0 + q
                    else:
                        q = ext[l] + co[3, l] * mean[0]
                    qs.append(q)
                us = []
                for k, q in zip(batch, qs):
                    a, b, c, d, km = scalars(co, v * G + k)
                    h = pltpu.roll(p, (125 - 8 * k) % 128, 1)
                    wv = jnp.where(is0, h, pltpu.roll(q, 1, 1))
                    ev = jnp.where(is127, h, pltpu.roll(q, 127, 1))
                    us.append(stencil(E, q, wv, ev, a, b, c, d))
                for k, u in zip(batch, us):
                    l = v * G + k
                    if last:
                        own[l] = u[0:R]
                    else:
                        ext[l] = u
                        total = total + u
            if not last:
                sums[0] = total
            if first:
                sums[3] = total0
            if after is not None:
                after(v, n)

        f.groups(group)

    def fold(x):
        for s in (8, 16, 32, 64):
            x = x + pltpu.roll(x, s, 1)
        return x

    def v_copy(src, dst, i):
        return pltpu.make_async_remote_copy(
            src_ref=src, dst_ref=dst, send_sem=v_ss.at[i], recv_sem=v_rs.at[i],
            device_id={"vert": other}, device_id_type=MESH,
        )

    def send0(f, sums, kk, vs, vr, i):
        for j in range(6):
            s = sums[j]
            vs[j, 0 : f.E, :] = s if j in (0, 3) else fold(s)
        vs[6, 0:8, :] = jnp.full((8, 128), kk, F32)
        cp = v_copy(vs, vr, i)
        cp.start()
        return cp

    def send1(f, sums, us, ur, slot, i):
        for j in range(3 if slot == 0 else 1):
            us[slot, j] = sums[j] if j == 0 else fold(sums[j])
        if slot == 1:
            cp = v_copy(us.at[slot, 0], ur.at[slot, 0], i)
        else:
            cp = v_copy(us.at[slot], ur.at[slot], i)
        cp.start()
        return cp

    def means0(f, vs, vr):
        inv = F32(1.0 / f.total)
        ksum = (vs[6, 0:1, :] + vr[6, 0:1, :]) * inv
        m0 = [(vs[3 + j] + vr[3 + j]) * inv for j in range(3)]
        m1 = [(vs[j] + vr[j]) * inv + ksum * m0[j] for j in range(3)]
        return m0, m1, ksum

    for side in range(2):
        x_copy(1 - side).wait_recv()
    for n in range(NR):
        for j in range(3):
            c_copy(n, j).wait_recv()

    one_pass(fa, ac, a_cl, a_own, a_ext, a_w, a_e, a_sum, None, first=True)
    a0 = send0(fa, a_sum, a_k, a_vs, a_vr, 0)
    one_pass(fo, oc, o_cl, o_own, o_ext, o_w, o_e, o_sum, None, first=True)
    o0 = send0(fo, o_sum, o_k, o_vs, o_vr, 1)

    def r_wait(k, carry):
        r_copy(k).wait_recv()
        return carry

    lax.fori_loop(1, peers, r_wait, 0)
    loads[2].wait()
    nbo = rem_ref.shape[1]
    subo = sub_iota(nbo)

    def entry(e, acc):
        s = listed(me, e, 0)
        dev = s // nba
        t = lax.rem(listed(me, e, 1), nbo)
        wi = listed(me, e, 2)

        def before(x, got):
            return jnp.where(listed(me, x, 0) // nba == dev, jnp.int32(1), got)

        second = jnp.int32(0)
        if isinstance(e, int):
            for x in range(e):
                second = before(x, second)
        else:
            second = lax.fori_loop(0, e, before, second)
        prod = jnp.dot(rr[dev].astype(BF16), wbuf[wi], preferred_element_type=F32)
        hit = subo == t
        out = []
        for f in range(flux_f):
            row = jnp.where(second == 1, prod[flux_f + f : flux_f + f + 1], prod[f : f + 1])
            out.append(acc[f] + jnp.where(hit, row, 0.0))
        return tuple(out)

    acc = tuple(jnp.zeros((nbo, 128), F32) for _ in range(flux_f))
    if entries <= 16:
        for e in range(entries):
            acc = entry(e, acc)
    else:
        acc = lax.fori_loop(0, entries, entry, acc)
    for f in range(flux_f):
        rem_ref[f] = acc[f]

    def keep(f, sums, ms):
        for j in range(3):
            sums[j] = ms[j]

    a0.wait()
    am0, am1, a_ks = means0(fa, a_vs, a_vr)
    for j in range(3):
        a_vs[j] = am0[j]
        a_vs[3 + j] = am1[j]
    one_pass(fa, ac, a_cl, a_own, a_ext, a_w, a_e, a_sum, a_vs.at[0:3])
    a1 = send1(fa, a_sum, a_us, a_ur, 0, 2)

    o0.wait()
    om0, om1, o_ks = means0(fo, o_vs, o_vr)
    for j in range(3):
        o_vs[j] = om0[j]
        o_vs[3 + j] = om1[j]
    one_pass(fo, oc, o_cl, o_own, o_ext, o_w, o_e, o_sum, o_vs.at[0:3])
    o1 = send1(fo, o_sum, o_us, o_ur, 0, 3)

    one_pass(fa, ac, a_cl, a_own, a_ext, a_w, a_e, a_sum, a_vs.at[3:6])
    a2 = send1(fa, a_sum, a_us, a_ur, 1, 4)
    one_pass(fo, oc, o_cl, o_own, o_ext, o_w, o_e, o_sum, o_vs.at[3:6])
    o2 = send1(fo, o_sum, o_us, o_ur, 1, 5)

    def mean2(f, us, ur, vs, ks):
        inv = F32(1.0 / f.total)
        for j in range(3):
            vs[j] = (us[0, j] + ur[0, j]) * inv + ks * vs[3 + j]

    def out_copies(own, hbm, base):
        def after(v, n):
            at = v * G
            pltpu.make_async_copy(own.at[pl.ds(at, n)], hbm.at[pl.ds(at, n)], out_sem.at[base + v]).start()

        return after

    a1.wait()
    mean2(fa, a_us, a_ur, a_vs, a_ks)
    one_pass(fa, ac, a_cl, a_own, a_ext, a_w, a_e, a_sum, a_vs.at[0:3], last=True, after=out_copies(a_own, ua_hbm, 0))
    o1.wait()
    mean2(fo, o_us, o_ur, o_vs, o_ks)
    one_pass(fo, oc, o_cl, o_own, o_ext, o_w, o_e, o_sum, o_vs.at[0:3], last=True, after=out_copies(o_own, uo_hbm, fa.V))
    a2.wait()
    o2.wait()
    ma_ref[...] = ((a_us[1, 0] + a_ur[1, 0]) * F32(1.0 / fa.total) + a_ks * a_vs[0])[0 : fa.R]
    mo_ref[...] = ((o_us[1, 0] + o_ur[1, 0]) * F32(1.0 / fo.total) + o_ks * o_vs[0])[0 : fo.R]

    for f, own, hbm, base in ((fa, a_own, ua_hbm, 0), (fo, o_own, uo_hbm, fa.V)):
        for v, n in f.chunks:
            at = v * G
            pltpu.make_async_copy(own.at[pl.ds(at, n)], hbm.at[pl.ds(at, n)], out_sem.at[base + v]).wait()
    for side in range(2):
        x_copy(side).wait_send()
    for n in range(NR):
        for j in range(3):
            c_copy(n, j).wait_send()
        for i in range(fa.V):
            z_copy(fa, n, i, 0).wait_send()
        for i in range(fo.V):
            z_copy(fo, n, i, oz).wait_send()

    def r_done(k, carry):
        r_copy(k).wait_send()
        return carry

    lax.fori_loop(1, peers, r_done, 0)


def body(H, C, KV, atm_state, atm_coeffs, ocean_state, ocean_coeffs, atm_flux, remap_weights, remap_list, ocean_mask):
    la, ra, _ = atm_state.shape
    lo, ro, _ = ocean_state.shape
    flux_f, nba, _ = atm_flux.shape
    entries = remap_list.shape[1]
    nbo = ocean_mask.shape[0]
    peers = H * C
    NR = 1 if C == 2 else 2
    remap_list = jnp.transpose(remap_list, (2, 0, 1))
    va, vo = (la + G - 1) // G, (lo + G - 1) // G
    fa = Field(la, ra, KV * la, 0, 0, 0, 0)
    fo = Field(lo, ro, KV * lo, va * ZG, va * ra, rup(va, 2) * 8, 0)
    zrows = (va + vo) * ZG
    xrows = va * ra + vo * ro
    crows = (rup(va, 2) + rup(vo, 2)) * 8
    V = pltpu.VMEM
    DMA = pltpu.SemaphoreType.DMA
    scratch = [
        V((la, ra, 128), F32), V((lo, ro, 128), F32),
        V((la, fa.E, 128), F32), V((lo, fo.E, 128), F32),
        V((va, fa.E, 128), F32), V((va, fa.E, 128), F32),
        V((vo, fo.E, 128), F32), V((vo, fo.E, 128), F32),
        V((va, 8, 128), F32), V((vo, 8, 128), F32),
        V((6, fa.E, 128), F32), V((6, fo.E, 128), F32),
        V(remap_weights.shape, BF16),
        V((zrows, 128), BF16), V((NR, zrows, 128), BF16),
        V((xrows, 128), F32), V((xrows, 128), BF16), V((2, xrows, 128), BF16),
        V((crows, 128), BF16), V((NR, 3, crows, 128), BF16),
        V((7, fa.E, 128), F32), V((7, fa.E, 128), F32),
        V((7, fo.E, 128), F32), V((7, fo.E, 128), F32),
        V((2, 3, fa.E, 128), F32), V((2, 3, fa.E, 128), F32),
        V((2, 3, fo.E, 128), F32), V((2, 3, fo.E, 128), F32),
        V((peers * 8, 128), F32), V((peers, 8, 128), F32), V((peers, 8, 128), F32),
        DMA((3,)), DMA((va + vo,)),
        DMA((NR, va + vo)), DMA((NR, va + vo)),
        DMA((2,)), DMA((2,)),
        DMA((NR, 3)), DMA((NR, 3)),
        DMA((6,)), DMA((6,)),
        DMA((peers,)), DMA((peers,)),
    ]
    anyspec = pl.BlockSpec(memory_space=pl.ANY)
    hbm = pl.BlockSpec(memory_space=pltpu.HBM)
    vspec = pl.BlockSpec(memory_space=pltpu.VMEM)
    sspec = pl.BlockSpec(memory_space=pltpu.SMEM)
    ua, uo, ma, mo, rem, ka, ko = pl.pallas_call(
        functools.partial(kernel, fa, fo, NR, H, C, flux_f, nba, entries),
        out_shape=(
            jax.ShapeDtypeStruct((la, ra, 128), F32),
            jax.ShapeDtypeStruct((lo, ro, 128), F32),
            jax.ShapeDtypeStruct((ra, 128), F32),
            jax.ShapeDtypeStruct((ro, 128), F32),
            jax.ShapeDtypeStruct((flux_f, nbo, 128), F32),
            jax.ShapeDtypeStruct((1, la), F32),
            jax.ShapeDtypeStruct((1, lo), F32),
        ),
        in_specs=[hbm, hbm, hbm, vspec, sspec, sspec, sspec],
        out_specs=(anyspec, anyspec, vspec, vspec, vspec, sspec, sspec),
        scratch_shapes=scratch,
        compiler_params=pltpu.CompilerParams(
            collective_id=0, has_side_effects=True, vmem_limit_bytes=32 * 1024 * 1024
        ),
    )(
        *[
            pltpu.with_memory_space_constraint(x, pltpu.HBM)
            for x in (
                atm_state, ocean_state, remap_weights, atm_flux, atm_coeffs, ocean_coeffs, remap_list
            )
        ]
    )
    return (
        ua + ka[0][:, None, None] * ma[None],
        uo + ko[0][:, None, None] * mo[None],
        rem * ocean_mask.astype(F32)[None],
    )


def solution(mesh):
    H, C, KV = mesh.shape["horiz"], mesh.shape["comp"], mesh.shape["vert"]
    return jax.shard_map(
        functools.partial(body, H, C, KV),
        mesh=mesh,
        in_specs=(
            P("vert", ("runs", "comp"), "horiz"),
            P(None, "vert"),
            P("vert", ("runs", "comp"), "horiz"),
            P(None, "vert"),
            P("vert", ("runs", "horiz", "comp"), None),
            P(),
            P(),
            P(("horiz", "comp"), None),
        ),
        out_specs=(
            P("vert", ("runs", "comp"), "horiz"),
            P("vert", ("runs", "comp"), "horiz"),
            P("vert", ("runs", "horiz", "comp"), None),
        ),
        check_vma=False,
    )
```
